32 devices in a mesh: view: 4 (over x, core), band: 8 (over z, y).
Axes of the slice: x: 2, y: 2, z: 4, core: 2. Of those that a mesh axis runs over, the one named last changes fastest.
Arguments:
- latents: bfloat16 [4, 2048, 1024], P('view', 'band'), may hold values from -170 to 170
- w_qkv: bfloat16 [1024, 3072], replicated, may hold values from -0.75 to 0.75
- w_out: bfloat16 [1024, 1024], replicated, may hold values from -0.1875 to 0.1875
- epipolar_bands: int32 [4, 8, 4], replicated, may hold values from -1 to 7, as said below
- object_token_mask: int32 [4, 2048], replicated, may hold values from 0 to 1, as said below
Outputs:
- updated: float32 [4, 2048, 1024], P('view', 'band')
The draws below stay inside these ranges and needn't reach their ends.
Inputs may be any that keep to these rules, and one draw needn't show every extreme that they name: epipolar_bands[v, b, w] is -1 where w is v or the epipolar lines miss view w; otherwise a band of view w within 2 bands of b. For every query band and every nonzero distance d, at most 2 views have band b + d listed, and some query band lists 2 views at one such distance. `object_token_mask`: the first token of every band is 1.
All inputs are finite; a program needn't handle non-finite values.
Results may differ from the reference program's by a relative error of at most 0.023.
Values may be sent and summed in bfloat16 or wider, within the bound.
No kernel may reach another device: no remote copies, remote signals or barrier semaphores. Data moves between devices by JAX's collectives and lax.ppermute only.
A program may use at most 128 MiB of HBM per device.

```python
import jax
import jax.numpy as jnp
from jax import lax

D = 1024
HEADS = 16
HEAD_DIM = 64
TOKENS_PER_BAND = 256
REACH = 2
MOST = 2
VIEW_COUNT = 4
ROW_BAND_COUNT = 8
TOKENS_VIEW = 2048


def draw_latents(key, part):
    key = jax.random.fold_in(key, 5)
    first = jax.random.fold_in(key, 0)
    values = jnp.clip(jax.random.normal(first, (VIEW_COUNT, TOKENS_VIEW, D), jnp.float32), -6.0, 6.0)
    return values.astype(jnp.bfloat16)


def draw_object_token_mask(key, part):
    key = jax.random.fold_in(key, 7)
    first, second = jax.random.split(key)
    level = jax.random.randint(first, (VIEW_COUNT, ROW_BAND_COUNT, 1), 1, 9)
    coin = jax.random.randint(second, (VIEW_COUNT, ROW_BAND_COUNT, TOKENS_PER_BAND), 0, 8)
    first_token = jnp.arange(TOKENS_PER_BAND)[None, None, :] == 0
    live = (coin < level) | first_token
    return jnp.where(live, 1, 0).astype(jnp.int32).reshape(VIEW_COUNT, TOKENS_VIEW)


def draw_epipolar_bands(key, part):
    key = jax.random.fold_in(key, 11)
    first, second = jax.random.split(key)
    view_numbers = jnp.arange(VIEW_COUNT, dtype=jnp.int32)
    band_ids = jnp.arange(ROW_BAND_COUNT, dtype=jnp.int32)[None, :, None]
    offsets = jax.random.randint(first, (VIEW_COUNT, ROW_BAND_COUNT, VIEW_COUNT), -REACH, REACH + 1)
    seen = jax.random.randint(second, (VIEW_COUNT, ROW_BAND_COUNT, VIEW_COUNT), 0, 4) > 0
    destination = jnp.clip(band_ids + offsets, 0, ROW_BAND_COUNT - 1)
    query_view = view_numbers[:, None, None]
    remote_view = view_numbers[None, None, :]
    forced_zone = (query_view == 0) & (band_ids == 0)
    forced = jnp.where((remote_view >= 1) & (remote_view <= MOST), 1, 0)
    destination = jnp.where(forced_zone, forced, destination)
    seen = jnp.where(forced_zone, True, seen)
    seen = seen & (query_view != remote_view)
    same = destination[..., :, None] == destination[..., None, :]
    earlier = view_numbers[None, :] < view_numbers[:, None]
    ranks = jnp.sum((same & seen[..., None, :] & earlier[None, None]).astype(jnp.int32), axis=-1)
    keep = seen & ((destination == band_ids) | (ranks < MOST))
    return jnp.where(keep, destination, -1).astype(jnp.int32)


def bell_draw(own_key, dims, scale, most, held_as=jnp.bfloat16):
    return jnp.clip(scale * jax.random.normal(own_key, dims, jnp.float32), -most, most).astype(held_as)


def setup_inputs(seed: int = 0) -> dict:
    seeds = jax.random.split(jax.random.key(seed), 6)
    latents = draw_latents(jax.random.fold_in(seeds[5], 71), 0)
    w_qkv = bell_draw(seeds[1], (D, 3 * D), (1.7 / D ** 0.5), 0.75)
    w_out = bell_draw(seeds[2], (D, D), D ** -0.5, 0.1875)
    epipolar_bands = draw_epipolar_bands(jax.random.fold_in(seeds[5], 71), 0)
    object_token_mask = draw_object_token_mask(jax.random.fold_in(seeds[5], 71), 0)
    return dict(latents=latents, w_qkv=w_qkv, w_out=w_out, epipolar_bands=epipolar_bands, object_token_mask=object_token_mask)


def attend(queries, key_rows, values, usable):
    count_of_rows = queries.shape[0]
    key_count = key_rows.shape[0]
    query_f = queries.astype(jnp.float32).reshape(count_of_rows, HEADS, HEAD_DIM)
    key_f = key_rows.astype(jnp.float32).reshape(key_count, HEADS, HEAD_DIM)
    value_f = values.astype(jnp.float32).reshape(key_count, HEADS, HEAD_DIM)
    scores = jnp.einsum("qhd,khd->hqk", query_f, key_f) * (HEAD_DIM ** -0.5)
    scores = jnp.where(usable[None, None, :], scores, -1e30)
    row_top = jnp.max(scores, axis=-1, keepdims=True)
    raised = jnp.exp(scores - row_top)
    attention = (raised / jnp.sum(raised, axis=-1, keepdims=True)).astype(jnp.bfloat16)
    blended = jnp.einsum("hqk,khd->qhd", attention.astype(jnp.float32), value_f)
    return blended.reshape(count_of_rows, HEADS * HEAD_DIM).astype(jnp.bfloat16)


def reference(latents, w_qkv, w_out, epipolar_bands, object_token_mask):
    width = latents.shape[2]
    projected = jnp.dot(latents.reshape(VIEW_COUNT * TOKENS_VIEW, width), w_qkv, preferred_element_type=jnp.float32).astype(jnp.bfloat16)
    projected = projected.reshape(VIEW_COUNT, ROW_BAND_COUNT, TOKENS_PER_BAND, 3 * width)
    active_flags = object_token_mask.reshape(VIEW_COUNT, ROW_BAND_COUNT, TOKENS_PER_BAND) > 0

    def one_band(flat_index):
        view_lookup = flat_index // ROW_BAND_COUNT
        band_at = flat_index % ROW_BAND_COUNT
        queries = projected[view_lookup, band_at, :, :width]
        slab_list = []
        active_list = []
        for step_off in (-1, 0, 1):
            destination = band_at + step_off
            clamped_index = jnp.clip(destination, 0, ROW_BAND_COUNT - 1).astype(jnp.int32)
            slab_list.append(projected[view_lookup, clamped_index, :, width:])
            active_list.append(active_flags[view_lookup, clamped_index] & (destination >= 0) & (destination < ROW_BAND_COUNT))
        for remote_view in range(VIEW_COUNT):
            destination = epipolar_bands[view_lookup, band_at, remote_view]
            clamped_index = jnp.clip(destination, 0, ROW_BAND_COUNT - 1).astype(jnp.int32)
            slab_list.append(projected[remote_view, clamped_index, :, width:])
            active_list.append(active_flags[remote_view, clamped_index] & (destination >= 0) & (view_lookup != remote_view))
        slabs = jnp.concatenate(slab_list, axis=0)
        usable = jnp.concatenate(active_list, axis=0)
        return attend(queries, slabs[:, :width], slabs[:, width:], usable)

    blended = lax.map(one_band, jnp.arange(VIEW_COUNT * ROW_BAND_COUNT, dtype=jnp.int32))
    blended = blended.reshape(VIEW_COUNT * TOKENS_VIEW, width)
    updated = latents.reshape(VIEW_COUNT * TOKENS_VIEW, width).astype(jnp.float32) + jnp.dot(blended, w_out, preferred_element_type=jnp.float32)
    return updated.reshape(VIEW_COUNT, TOKENS_VIEW, width)
```

```python
import functools

import jax
import jax.numpy as jnp
from jax import lax
from jax.experimental import pallas as pl
from jax.experimental.pallas import tpu as pltpu
from jax.sharding import PartitionSpec as P

HEADS = 16
HEAD_DIM = 64
PAIR = 2 * HEAD_DIM
REACH = 2
DEAD = -1e30
TILE = 256

NT = (((1,), (1,)), ((), ()))


def vmem():
    return pl.BlockSpec(memory_space=pltpu.VMEM)


def select_kernel(choice, *refs):
    window, (direct, across, sem) = refs[:5], refs[5:]
    slots = [direct.at[0]] + [across.at[i] for i in range(across.shape[0])]
    for slot, out in enumerate(slots):
        for at, source in enumerate(window):

            @pl.when(choice[slot] == at)
            def _():
                pltpu.make_async_copy(source, out, sem.at[slot]).start()

    for slot, out in enumerate(slots):
        pltpu.make_async_copy(window[0], out, sem.at[slot]).wait()


def select(choice, window, others):
    tokens, width = window[0].shape
    dtype = window[0].dtype
    return pl.pallas_call(
        select_kernel,
        out_shape=(
            jax.ShapeDtypeStruct((1, tokens, width), dtype),
            jax.ShapeDtypeStruct((others - 1, tokens, width), dtype),
        ),
        in_specs=[pl.BlockSpec(memory_space=pltpu.SMEM)] + [pl.BlockSpec(memory_space=pl.ANY)] * 5,
        out_specs=(pl.BlockSpec(memory_space=pl.ANY),) * 2,
        scratch_shapes=[pltpu.SemaphoreType.DMA((others,))],
        name="select_blocks",
    )(choice, *window)


def project_keys(blocks, w_k, w_v_t, keys, values_t):
    width = w_k.shape[1]
    row = 0
    for block in blocks:
        count = block.shape[0]
        x = block[...]
        for col in range(0, width, TILE):
            cols = pl.ds(col, TILE)
            keys[pl.ds(row, count), cols] = jnp.dot(
                x, w_k[:, cols], preferred_element_type=jnp.float32
            ).astype(jnp.bfloat16)
            values_t[cols, pl.ds(row, count)] = lax.dot_general(
                w_v_t[cols, :], x, NT, preferred_element_type=jnp.float32
            ).astype(jnp.bfloat16)
        row += count


def head_part(head, queries, keys, values_t, bias):
    lanes = pl.ds((head // 2) * PAIR, PAIR)
    scores = jnp.dot(keys[:, lanes], queries[head], preferred_element_type=jnp.float32)
    scores = scores + bias
    top = jnp.max(scores, axis=0, keepdims=True)
    raised = jnp.exp(scores - top)
    total = jnp.sum(raised, axis=0, keepdims=True)
    mixed = jnp.dot(
        values_t[pl.ds(head * HEAD_DIM, HEAD_DIM), :],
        raised.astype(jnp.bfloat16),
        preferred_element_type=jnp.float32,
    )
    return top, total, mixed


def wide_bias(bias_ref, count):
    bias = bias_ref[...]
    return jnp.concatenate([bias] * (count // bias.shape[1]), axis=1)


def near_kernel(own, side, diag, bias, w_q_t, w_k, w_v_t, queries, top, total, mixed, keys, values_t):
    count = own.shape[0]
    scale = HEAD_DIM**-0.5
    x = own[...]
    empty = jnp.zeros((HEAD_DIM, count), jnp.bfloat16)
    for head in range(HEADS):
        rows = pl.ds(head * HEAD_DIM, HEAD_DIM)
        q = lax.dot_general(w_q_t[rows, :], x, NT, preferred_element_type=jnp.float32)
        q = (q.astype(jnp.bfloat16).astype(jnp.float32) * scale).astype(jnp.bfloat16)
        parts = [q, empty] if head % 2 == 0 else [empty, q]
        queries[head] = jnp.concatenate(parts, axis=0)
    project_keys([own, side, diag], w_k, w_v_t, keys, values_t)
    live = wide_bias(bias, count)
    for head in range(HEADS):
        t, s, o = head_part(head, queries, keys, values_t, live)
        top[head] = t
        total[head] = s
        mixed[pl.ds(head * HEAD_DIM, HEAD_DIM), :] = o


def far_kernel(
    blocks, own, bias, w_k, w_v_t, w_out, queries, top, total, mixed, out, keys, values_t, blended
):
    count = own.shape[0]
    project_keys([blocks.at[i] for i in range(blocks.shape[0])], w_k, w_v_t, keys, values_t)
    live = wide_bias(bias, count)
    for head in range(HEADS):
        rows = pl.ds(head * HEAD_DIM, HEAD_DIM)
        t, s, o = head_part(head, queries, keys, values_t, live)
        before = top[head]
        peak = jnp.maximum(before, t)
        old, new = jnp.exp(before - peak), jnp.exp(t - peak)
        whole = old * total[head] + new * s
        o = (old * mixed[rows, :] + new * o) / whole
        blended[rows, :] = o.astype(jnp.bfloat16)
    flat = blended[...].T
    for col in range(0, w_out.shape[1], TILE):
        cols = pl.ds(col, TILE)
        out[:, cols] = own[:, cols].astype(jnp.float32) + jnp.dot(
            flat, w_out[:, cols], preferred_element_type=jnp.float32
        )


def near_part(own, side, diag, bias, w_q_t, w_k, w_v_t):
    count, width = own.shape
    keys = bias.shape[0]
    flops = 2 * count * width * width * 7 + 4 * count * keys * width * 4
    return pl.pallas_call(
        near_kernel,
        out_shape=(
            jax.ShapeDtypeStruct((HEADS, PAIR, count), jnp.bfloat16),
            jax.ShapeDtypeStruct((HEADS, 1, count), jnp.float32),
            jax.ShapeDtypeStruct((HEADS, 1, count), jnp.float32),
            jax.ShapeDtypeStruct((width, count), jnp.float32),
        ),
        in_specs=[vmem()] * 7,
        out_specs=(vmem(),) * 4,
        scratch_shapes=[
            pltpu.VMEM((keys, width), jnp.bfloat16),
            pltpu.VMEM((width, keys), jnp.bfloat16),
        ],
        compiler_params=pltpu.CompilerParams(vmem_limit_bytes=40 * 2**20),
        cost_estimate=pl.CostEstimate(
            flops=flops, bytes_accessed=10 * 2**20, transcendentals=count * keys * HEADS
        ),
        name="near_part",
    )(own, side, diag, bias, w_q_t, w_k, w_v_t)


def far_part(blocks, own, bias, w_k, w_v_t, w_out, queries, top, total, mixed):
    count, width = own.shape
    keys = bias.shape[0]
    flops = 2 * count * width * width * (2 * blocks.shape[0] + 1) + 4 * count * keys * width * 4
    return pl.pallas_call(
        far_kernel,
        out_shape=jax.ShapeDtypeStruct((count, width), jnp.float32),
        in_specs=[vmem()] * 10,
        out_specs=vmem(),
        scratch_shapes=[
            pltpu.VMEM((keys, width), jnp.bfloat16),
            pltpu.VMEM((width, keys), jnp.bfloat16),
            pltpu.VMEM((width, count), jnp.bfloat16),
        ],
        compiler_params=pltpu.CompilerParams(vmem_limit_bytes=40 * 2**20),
        cost_estimate=pl.CostEstimate(
            flops=flops, bytes_accessed=10 * 2**20, transcendentals=count * keys * HEADS
        ),
        name="far_part",
    )(blocks, own, bias, w_k, w_v_t, w_out, queries, top, total, mixed)


def body(latents, w_qkv, w_out, epipolar_bands, object_token_mask):
    views = lax.axis_size("view")
    bands = lax.axis_size("band")
    view = lax.axis_index("view")
    band = lax.axis_index("band")
    own = latents[0]
    count, width = own.shape

    up = lax.ppermute(own, "band", [(i, i + REACH) for i in range(bands - REACH)])
    down = lax.ppermute(own, "band", [(i + REACH, i) for i in range(bands - REACH)])
    side = lax.ppermute(own, "band", [(i, i ^ 1) for i in range(bands)])
    inner = range(1, bands - 1)
    diag = lax.ppermute(own, "band", [(i, i + 1 if i % 2 else i - 1) for i in inner])

    even = band % 2 == 0
    side_step = jnp.where(even, 1, -1)
    distances = jnp.stack([-REACH, REACH, side_step, -side_step, 0]).astype(jnp.int32)

    partners = [view ^ 1] + [view ^ k for j in range(2, views, 2) for k in (j, j + 1)]
    partners = jnp.stack(partners).astype(jnp.int32)
    wanted = epipolar_bands[partners, band, view]
    wanted = jnp.where(wanted >= 0, wanted - band, 0)
    choice = jnp.argmax(wanted[:, None] == distances[None, :], axis=1).astype(jnp.int32)
    direct, across = select(choice, [up, down, side, diag, own], views - 1)

    arrived = [direct]
    kept = []
    for at, k in enumerate(range(2, views, 2)):
        both = lax.ppermute(
            across[2 * at : 2 * at + 2], "view", [(i, i ^ k) for i in range(views)]
        )
        kept.append(both[:1])
        arrived.append(both[1:])
    swapped = lax.ppermute(
        jnp.concatenate(arrived, axis=0), "view", [(i, i ^ 1) for i in range(views)]
    )
    blocks = jnp.concatenate([swapped] + kept, axis=0)
    far_views = [view ^ 1] + [view ^ 1 ^ k for k in range(2, views, 2)]
    far_views += [view ^ k for k in range(2, views, 2)]
    far_views = jnp.stack(far_views).astype(jnp.int32)

    flags = object_token_mask.reshape(views * bands, count)
    listed = epipolar_bands[view, band, far_views]
    near_bands = jnp.stack([band, band + side_step, band - side_step])
    all_bands = jnp.concatenate([near_bands, listed]).astype(jnp.int32)
    all_views = jnp.concatenate([jnp.stack([view] * 3).astype(jnp.int32), far_views])
    exists = (all_bands >= 0) & (all_bands < bands)
    live = flags[all_views * bands + jnp.clip(all_bands, 0, bands - 1)]
    live = (live > 0) & exists[:, None]
    bias = jnp.where(live, 0.0, DEAD).astype(jnp.float32).reshape(-1, 1)
    bias = jnp.broadcast_to(bias, (bias.shape[0], 128))

    w_q_t = w_qkv[:, :width].T
    w_k = w_qkv[:, width : 2 * width]
    w_v_t = w_qkv[:, 2 * width :].T

    queries, top, total, mixed = near_part(
        own, side, diag, bias[: 3 * count], w_q_t, w_k, w_v_t
    )
    updated = far_part(
        blocks, own, bias[3 * count :], w_k, w_v_t, w_out, queries, top, total, mixed
    )
    return updated[None]


def solution(mesh):
    placed = (P("view", "band", None), P(), P(), P(), P())
    return jax.shard_map(
        body, mesh=mesh, in_specs=placed, out_specs=P("view", "band", None), check_vma=False
    )
```
